128 devices in a mesh: grp: 16 (over y, z), tri: 8 (over x, core).
Axes of the slice: x: 4, y: 4, z: 4, core: 2. Of those that a mesh axis runs over, the one named last changes fastest.
Arguments:
- samples: bfloat16 [2048, 647168], P(('grp', 'tri')), may hold values from -6 to 6
- fir_taps: float32 [16, 8192], replicated, may hold values from -1.5 to 1.5
- channel_group: int32 [512], replicated, may hold values from 0 to 15, as said below
- tile_pairs: int32 [2, 136], P(None, 'tri'), may hold values from 0 to 15, as said below
Outputs:
- visibilities: bfloat16 [64, 136, 2, 128, 128], P('grp', 'tri')
The draws below stay inside these ranges and needn't reach their ends.
Inputs may be any that keep to these rules, and one draw needn't show every extreme that they name: `channel_group`: each group is named by exactly 32 channels. `tile_pairs`: every pair of blocks with row <= column appears in exactly one slot.
All inputs are finite; a program needn't handle non-finite values.
Results may differ from the reference program's by a relative error of at most 0.0071.
Values may be sent and summed in bfloat16 or wider, within the bound.
A program may use at most 192 MiB of HBM per device.

```python
import math
import jax
import jax.numpy as jnp
import numpy as np
from jax import lax

DISHES = 2048
NFFT = 8192
TAPS = 16
BLOCK = 128
FIRST_CH = 1024
CH_GRP = 32
FAVG = 8
SPECTRA = 64
CHANNELS = 512
NBLK = 16
NTILE = 136


def draw_channel_group(key, part):
    key = jax.random.fold_in(key, 11)
    shuffled = jax.random.permutation(key, CHANNELS)
    return (shuffled // CH_GRP).astype(jnp.int32)


def draw_tile_pairs(key, part):
    key = jax.random.fold_in(key, 23)
    upper_rows, upper_cols = np.triu_indices(NBLK)
    shuffled = jax.random.permutation(key, NTILE)
    tile_rows = jnp.asarray(upper_rows.astype(np.int32))[shuffled]
    tile_cols = jnp.asarray(upper_cols.astype(np.int32))[shuffled]
    return jnp.stack([tile_rows, tile_cols]).astype(jnp.int32)


def level_of(own_key, extent, split, least, top_value):
    factor_of, own = 1.0, jax.random.fold_in(own_key, 6)
    for dim, parts in split:
        heights = jnp.exp(jax.random.uniform(jax.random.fold_in(own, dim), (parts,), jnp.float32, least / len(split), top_value / len(split)))
        factor_of = factor_of * jnp.repeat(heights, extent[dim] // parts).reshape([-1 if axis == dim else 1 for axis in range(len(extent))])
    return factor_of


def noise(key, extent, width, limit, pieces=(), kind=jnp.bfloat16):
    values = jax.random.normal(key, extent, jnp.float32) * width
    if len(pieces) > 0:
        values = level_of(key, extent, pieces, -0.22, 0.18) * values
    return jnp.clip(values, min=-limit, max=limit).astype(kind)


def setup_inputs(seed: int = 0) -> dict:
    streams_of = jax.random.split(jax.random.key(seed), 5)
    samples = noise(streams_of[0], (DISHES, (SPECTRA + TAPS - 1) * NFFT), 1.0, 6.0, ((0, 128),))
    fir_taps = noise(streams_of[1], (TAPS, NFFT), TAPS ** -0.5, 1.5, (), jnp.float32)
    channel_group = draw_channel_group(jax.random.fold_in(streams_of[4], 71), 0)
    tile_pairs = draw_tile_pairs(jax.random.fold_in(streams_of[4], 71), 0)
    return {"samples": samples, "fir_taps": fir_taps, "channel_group": channel_group, "tile_pairs": tile_pairs}


def dft_table(channels):
    sample_index = jnp.arange(NFFT, dtype=jnp.int32)[:, None]
    channel_index = FIRST_CH + jnp.arange(channels, dtype=jnp.int32)[None, :]
    phases = (sample_index * channel_index % NFFT).astype(jnp.float32)
    angles = phases * (2.0 * math.pi / NFFT)
    norm_scale = 1.0 / math.sqrt(NFFT)
    return jnp.concatenate([jnp.cos(angles) * norm_scale, -jnp.sin(angles) * norm_scale], axis=1).astype(jnp.bfloat16)

def polyphase(frames, fir_taps):
    spectra_count = frames.shape[1] - TAPS + 1
    accumulated = jnp.zeros((frames.shape[0], spectra_count, NFFT), jnp.float32)
    for tap_index in range(TAPS):
        accumulated = accumulated + frames[:, tap_index:tap_index + spectra_count].astype(jnp.float32) * fir_taps[tap_index]
    return accumulated.astype(jnp.bfloat16)

def reference(samples, fir_taps, channel_group, tile_pairs):
    phases_table = dft_table(CHANNELS)
    frames = samples.reshape(NBLK, BLOCK, SPECTRA + TAPS - 1, NFFT)

    def channelize(dish_block):
        filtered = polyphase(dish_block, fir_taps)
        flat_spectra = jnp.dot(filtered.reshape(-1, NFFT), phases_table, preferred_element_type=jnp.float32)
        return flat_spectra.astype(jnp.bfloat16).reshape(BLOCK, SPECTRA, 2, CHANNELS)
    spectra = lax.map(channelize, frames).reshape(DISHES, SPECTRA, 2, CHANNELS)
    voltages = jnp.transpose(spectra, (3, 0, 2, 1)).reshape(CHANNELS, DISHES, 2 * SPECTRA)
    same_group = channel_group[:, None] == channel_group[None, :]
    earlier = jnp.arange(CHANNELS)[None, :] < jnp.arange(CHANNELS)[:, None]
    channel_rank = lax.optimization_barrier(jnp.sum(same_group & earlier, axis=1)).astype(jnp.int32)
    position = (channel_group * CH_GRP + channel_rank).astype(jnp.int32)
    channel_order = jnp.zeros((CHANNELS,), jnp.int32).at[position].set(jnp.arange(CHANNELS, dtype=jnp.int32))
    channel_sets = channel_order.reshape(CHANNELS // FAVG, FAVG)
    tile_rows = tile_pairs[0]
    tile_cols = tile_pairs[1]

    def correlate(channel_set):
        channel_data = voltages[channel_set].reshape(FAVG, NBLK, BLOCK, 2 * SPECTRA)
        turned = jnp.concatenate([channel_data[..., SPECTRA:], -channel_data[..., :SPECTRA]], axis=3)
        row_blocks = jnp.concatenate([channel_data[:, tile_rows], turned[:, tile_rows]], axis=2).astype(jnp.float32)
        col_blocks = channel_data[:, tile_cols].astype(jnp.float32)
        products = jnp.einsum('qtis,qtjs->tij', row_blocks, col_blocks, precision=lax.Precision.HIGHEST)
        return (products * (1.0 / (SPECTRA * FAVG))).reshape(NTILE, 2, BLOCK, BLOCK).astype(jnp.bfloat16)
    return lax.map(correlate, channel_sets)
```

```python
import math

import jax
import jax.numpy as jnp
import numpy as np
from jax import lax
from jax.experimental import pallas as pl
from jax.experimental.pallas import tpu as pltpu
from jax.sharding import PartitionSpec as P

NFFT = 8192
TAPS = 16
BLOCK = 128
FIRST_CH = 1024
CHANNELS = 512
CH_GRP = 32
FAVG = 8
SPECTRA = 64
NBLK = 16
DISH = 16
GROUPS = 16
TRI = 8
ROWS = CH_GRP // FAVG
FSTEP = 8
CHUNKS = SPECTRA // FSTEP
MROWS = FSTEP * DISH
RADIX = 8
SUB = NFFT // RADIX
RESIDUES = (0, 4, 1, 7, 2, 6, 3, 5)
MESH = pl.DeviceIdType.MESH


def twiddle_tables():
    n = np.arange(SUB, dtype=np.int64)[:, None]
    k2 = np.arange(CHANNELS // RADIX, dtype=np.int64)[None, :]
    scale = 1.0 / math.sqrt(NFFT)
    tables = np.zeros((4, 2 * SUB, 256), np.float64)
    for pair in range(4):
        for which in range(2):
            residue = RESIDUES[2 * pair + which]
            channel = FIRST_CH + RADIX * k2 + residue
            angle = ((n * channel) % NFFT) * (2.0 * math.pi / NFFT)
            cos, sin = np.cos(angle) * scale, np.sin(angle) * scale
            lo = which * 128
            if pair == 0:
                rows = slice(which * SUB, (which + 1) * SUB)
                tables[pair, rows, lo : lo + 64] = cos
                tables[pair, rows, lo + 64 : lo + 128] = -sin
            else:
                sign = 1.0 if which == 0 else -1.0
                tables[pair, :SUB, lo : lo + 64] = cos
                tables[pair, SUB:, lo : lo + 64] = -sign * sin
                tables[pair, :SUB, lo + 64 : lo + 128] = -sin
                tables[pair, SUB:, lo + 64 : lo + 128] = -sign * cos
    return tables.astype(jnp.bfloat16)


def al(x):
    return pl.multiple_of(x, 128)


def channelize_kernel(
    samples, fir, tables, group_row, group_col, volts,
    xs, wt, perm, fbuf, planes, spec, send,
    x_sem, w_sem, own_sem, a2a_s, a2a_r, dir_s, dir_r, fwd_s, fwd_r, sib_s, sib_r,
):
    grp, tri = lax.axis_index("grp"), lax.axis_index("tri")
    gy, gz = grp // 4, lax.rem(grp, 4)
    cx, core = tri // 2, lax.rem(tri, 2)

    def group_at(dy, dz):
        return lax.rem(gy + dy, 4) * 4 + lax.rem(gz + dz, 4)

    def tri_at(dx):
        return lax.rem(cx + dx, 4) * 2 + core

    partners = [group_at(dy, dz) for dy in range(4) for dz in range(4) if (dy, dz) != (0, 0)]
    right, left, across = tri_at(1), tri_at(3), tri_at(2)
    sibling = cx * 2 + (1 - core)

    def frames_copy(i, count):
        cols = pl.ds(al(i * (FSTEP * NFFT)), count * NFFT)
        return pltpu.make_async_copy(samples.at[:, cols], xs.at[:, cols], x_sem.at[i])

    for i in range(3):
        frames_copy(i, FSTEP).start()
    table_copy = pltpu.make_async_copy(tables, wt, w_sem)
    table_copy.start()

    barrier = pltpu.get_barrier_semaphore()
    for p in partners:
        pl.semaphore_signal(barrier, inc=1, device_id=(p, tri), device_id_type=MESH)
    for t in (right, left, sibling):
        pl.semaphore_signal(barrier, inc=1, device_id=(grp, t), device_id_type=MESH)

    def number(shape, axis):
        i = lax.broadcasted_iota(jnp.int32, shape, axis)
        slot, k2 = i >> 6, i & 63
        residue = jnp.zeros_like(i)
        for s, r in enumerate(RESIDUES):
            residue = jnp.where(slot == s, r, residue)
        return k2 * RADIX + residue

    for piece in range(8):
        rows = pl.ds(piece * 64, 64)
        gcol = group_col[rows, :]
        shape = (64, CHANNELS)
        c_col = lax.broadcasted_iota(jnp.int32, shape, 0) * RADIX + RESIDUES[piece]
        hit = (gcol == group_row[...]) & (number(shape, 1) < c_col)
        rank = jnp.sum(hit.astype(jnp.int32), axis=1, keepdims=True)
        dst = (gcol >> 1) * 128 + (gcol & 1) * 32 + (rank >> 3) * 8 + (rank & 7)
        lane = lax.broadcasted_iota(jnp.int32, (64, 1024), 1)
        for part in range(2):
            one = (lane == dst + part * 64).astype(jnp.float32).astype(jnp.bfloat16)
            perm[pl.ds(piece * 128 + part * 64, 64), :] = one

    pl.semaphore_wait(barrier, len(partners) + 3)
    table_copy.wait()

    def a2a_copy(j, i):
        p = partners[i]
        return pltpu.make_async_remote_copy(
            src_ref=send.at[j, p], dst_ref=volts.at[j, tri, grp],
            send_sem=a2a_s.at[j], recv_sem=a2a_r.at[j],
            device_id=(p, tri), device_id_type=MESH)

    def own_copy(j):
        return pltpu.make_async_copy(send.at[j, grp], volts.at[j, tri, grp], own_sem.at[j])

    def part_copy(j, t, half, to, ssem, rsem):
        ref = volts.at[j, t] if half is None else volts.at[j, t, pl.ds(half * 8, 8)]
        return pltpu.make_async_remote_copy(
            src_ref=ref, dst_ref=ref, send_sem=ssem, recv_sem=rsem,
            device_id=(grp, to), device_id_type=MESH)

    def direct(j, way):
        return part_copy(j, tri, None, (right, left)[way], dir_s.at[way, j], dir_r.at[way, j])

    def forward(j, way):
        return part_copy(j, (left, right)[way], way, (right, left)[way], fwd_s.at[way, j], fwd_r.at[way, j])

    def share(j, which):
        return part_copy(j, (tri, left, right, across)[which], None, sibling, sib_s.at[which, j], sib_r.at[which, j])

    def stage_direct(j):
        own_copy(j).wait()
        some = volts.at[j, tri, pl.ds(0, GROUPS - 1)]
        pltpu.make_async_copy(some, some, a2a_r.at[j]).wait()
        for way in range(2):
            direct(j, way).start()
        share(j, 0).start()

    def stage_forward(j):
        for way in range(2):
            direct(j, way).wait_recv()
            forward(j, way).start()
        share(j, 1).start()
        share(j, 2).start()

    def stage_across(j):
        for way in range(2):
            forward(j, way).wait_recv()
        share(j, 3).start()

    half_root = math.sqrt(0.5)
    lane = lax.broadcasted_iota(jnp.int32, (DISH, 128), 1)

    def filter_tile(j, i):
        for n1 in range(RADIX):
            off = n1 * SUB + i * 128
            coef = [fir[pl.ds(t, 1), pl.ds(al(off), 128)] for t in range(TAPS)]
            acc = [None] * FSTEP
            for fr in range(FSTEP + TAPS - 1):
                x = xs[:, pl.ds(al((j * FSTEP + fr) * NFFT + off), 128)].astype(jnp.float32)
                for f in range(max(0, fr - TAPS + 1), min(FSTEP - 1, fr) + 1):
                    term = x * coef[fr - f]
                    acc[f] = term if acc[f] is None else acc[f] + term
                    if fr - f == TAPS - 1:
                        fbuf[n1, pl.ds(f * DISH, DISH), :] = acc[f]
        for f in range(FSTEP):
            rows = pl.ds(f * DISH, DISH)
            v = [fbuf[n1, rows, :] for n1 in range(RADIX)]
            a = [v[k] + v[k + 4] for k in range(4)]
            b = [v[k] - v[k + 4] for k in range(4)]
            even, odd = a[0] + a[2], a[1] + a[3]
            diff = (b[1] - b[3]) * half_root
            total = (b[1] + b[3]) * half_root
            out = (even + odd, even - odd, b[0] + diff, b[2] + total,
                   a[0] - a[2], a[1] - a[3], b[0] - diff, total - b[2])
            for k in range(RADIX):
                planes[rows, pl.ds(al(k * SUB + i * 128), 128)] = out[k].astype(jnp.bfloat16)

    def transform(j):
        for p in range(4):
            spec[:, p * 256 : (p + 1) * 256] = jnp.dot(
                planes[:, p * 2048 : (p + 1) * 2048], wt[p], preferred_element_type=jnp.float32
            ).astype(jnp.bfloat16)
        for blk in range(8):
            got = jnp.dot(spec[...], perm[:, blk * 128 : (blk + 1) * 128], preferred_element_type=jnp.float32)
            t = [got[f * DISH : (f + 1) * DISH] for f in range(FSTEP)]
            for bit in range(3):
                step = 1 << bit
                odd = (lane >> (3 + bit)) & 1 == 1
                new = list(t)
                for k in range(FSTEP):
                    if not k & step:
                        up = pltpu.roll(t[k + step], 8 * step, 1)
                        down = pltpu.roll(t[k], 128 - 8 * step, 1)
                        new[k] = jnp.where(odd, up, t[k])
                        new[k + step] = jnp.where(odd, t[k + step], down)
                t = new
            for k in range(FSTEP):
                send[j, blk * 2 + k // 4, k % 4] = t[k].astype(jnp.bfloat16)

    def step(s, carry):
        @pl.when(s < CHUNKS)
        def _():
            @pl.when(s + 3 < CHUNKS + 1)
            def _():
                frames_copy(s + 3, FSTEP).start()

            @pl.when(s + 3 == CHUNKS + 1)
            def _():
                frames_copy(CHUNKS + 1, FSTEP - 1).start()

            @pl.when(s == 0)
            def _():
                frames_copy(0, FSTEP).wait()
                frames_copy(1, FSTEP).wait()

            @pl.when(s + 2 < CHUNKS + 1)
            def _():
                frames_copy(s + 2, FSTEP).wait()

            @pl.when(s + 2 == CHUNKS + 1)
            def _():
                frames_copy(CHUNKS + 1, FSTEP - 1).wait()

            def tile(i, c):
                filter_tile(s, i)
                return c

            lax.fori_loop(0, SUB // 128, tile, 0)
            transform(s)
            for i in range(GROUPS - 1):
                a2a_copy(s, i).start()
            own_copy(s).start()

        @pl.when((s >= 1) & (s <= CHUNKS))
        def _():
            stage_direct(s - 1)

        @pl.when((s >= 2) & (s <= CHUNKS + 1))
        def _():
            stage_forward(s - 2)

        @pl.when(s >= 3)
        def _():
            stage_across(s - 3)

        return carry

    lax.fori_loop(0, CHUNKS + 3, step, 0)

    def finish(j, carry):
        some = send.at[j, pl.ds(0, GROUPS - 1)]
        pltpu.make_async_copy(some, some, a2a_s.at[j]).wait()
        for way in range(2):
            direct(j, way).wait_send()
            forward(j, way).wait_send()
        for which in range(4):
            share(j, which).wait()
        return carry

    lax.fori_loop(0, CHUNKS, finish, 0)


def channelize(samples, fir_taps, tables, group_row, group_col):
    dma = pltpu.SemaphoreType.DMA
    any_spec = pl.BlockSpec(memory_space=pl.ANY)
    vmem = pl.BlockSpec(memory_space=pltpu.VMEM)
    return pl.pallas_call(
        channelize_kernel,
        out_shape=jax.ShapeDtypeStruct((CHUNKS, TRI, NBLK, ROWS, DISH, 128), jnp.bfloat16),
        in_specs=[any_spec, vmem, any_spec, vmem, vmem],
        out_specs=any_spec,
        scratch_shapes=[
            pltpu.VMEM(samples.shape, jnp.bfloat16),
            pltpu.VMEM(tables.shape, jnp.bfloat16),
            pltpu.VMEM((1024, 1024), jnp.bfloat16),
            pltpu.VMEM((RADIX, MROWS, 128), jnp.float32),
            pltpu.VMEM((MROWS, NFFT), jnp.bfloat16),
            pltpu.VMEM((MROWS, 1024), jnp.bfloat16),
            pltpu.VMEM((CHUNKS, GROUPS, ROWS, DISH, 128), jnp.bfloat16),
            dma((CHUNKS + 2,)), dma, dma((CHUNKS,)), dma((CHUNKS,)), dma((CHUNKS,)),
            dma((2, CHUNKS)), dma((2, CHUNKS)), dma((2, CHUNKS)), dma((2, CHUNKS)),
            dma((4, CHUNKS)), dma((4, CHUNKS)),
        ],
        compiler_params=pltpu.CompilerParams(
            collective_id=0, has_side_effects=True, vmem_limit_bytes=58 << 20),
        name="channelize",
    )(samples, fir_taps, tables, group_row, group_col)


def correlate_kernel(pairs, volts, out, rows, turned):
    lane = lax.broadcasted_iota(jnp.int32, (BLOCK, 128), 1)
    for j in range(CHUNKS):
        cols = pl.ds(j * 128, 128)

        def arrange(b, c):
            v = volts[j, :, b, 0].reshape(BLOCK, 128)
            rows[b, :, cols] = v
            v = v.astype(jnp.float32)
            v = jnp.where(lane < 64, -1.0, 1.0) * pltpu.roll(v, 64, 1)
            turned[b, :, cols] = v.astype(jnp.bfloat16)
            return c

        lax.fori_loop(0, NBLK, arrange, 0)

    def tile(s, c):
        a, b = pairs[0, s], pairs[1, s]
        dims = (((1,), (1,)), ((), ()))
        for part, ref in enumerate((rows, turned)):
            got = lax.dot_general(rows[a], ref[b], dims, preferred_element_type=jnp.float32)
            out[0, s, part] = (got * (1.0 / (SPECTRA * FAVG))).astype(jnp.bfloat16)
        return c

    lax.fori_loop(0, out.shape[1], tile, 0)


def correlate(tile_pairs, volts):
    slots = tile_pairs.shape[1]
    return pl.pallas_call(
        correlate_kernel,
        grid_spec=pltpu.PrefetchScalarGridSpec(
            num_scalar_prefetch=1,
            grid=(ROWS,),
            in_specs=[pl.BlockSpec((CHUNKS, TRI, NBLK, 1, DISH, 128), lambda o, _: (0, 0, 0, o, 0, 0))],
            out_specs=pl.BlockSpec((1, slots, 2, BLOCK, BLOCK), lambda o, _: (o, 0, 0, 0, 0)),
            scratch_shapes=[
                pltpu.VMEM((NBLK, BLOCK, CHUNKS * 128), jnp.bfloat16),
                pltpu.VMEM((NBLK, BLOCK, CHUNKS * 128), jnp.bfloat16),
            ],
        ),
        out_shape=jax.ShapeDtypeStruct((ROWS, slots, 2, BLOCK, BLOCK), jnp.bfloat16),
        compiler_params=pltpu.CompilerParams(vmem_limit_bytes=58 << 20),
        name="correlate",
    )(tile_pairs, volts)


def shards(samples, fir_taps, channel_group, tile_pairs):
    order = np.concatenate([np.arange(r, CHANNELS, RADIX) for r in RESIDUES])
    by_residue = channel_group[order]
    volts = channelize(
        samples, fir_taps, jnp.asarray(twiddle_tables()), by_residue[None, :], by_residue[:, None]
    )
    return correlate(tile_pairs, volts)


def solution(mesh):
    in_specs = (P(("grp", "tri"), None), P(), P(), P(None, "tri"))
    out_specs = P("grp", "tri", None, None, None)
    return jax.shard_map(shards, mesh=mesh, in_specs=in_specs, out_specs=out_specs, check_vma=False)
```

```python
import math

import jax
import jax.numpy as jnp
import numpy as np
from jax import lax
from jax.experimental import pallas as pl
from jax.experimental.pallas import tpu as pltpu
from jax.sharding import PartitionSpec as P

NFFT = 8192
TAPS = 16
BLOCK = 128
FIRST_CH = 1024
CHANNELS = 512
CH_GRP = 32
FAVG = 8
SPECTRA = 64
NBLK = 16
DISH = 16
GROUPS = 16
TRI = 8
ROWS = CH_GRP // FAVG
FSTEP = 8
CHUNKS = SPECTRA // FSTEP
MROWS = FSTEP * DISH
RING = 4
RADIX = 8
SUB = NFFT // RADIX
RESIDUES = (0, 4, 1, 7, 2, 6, 3, 5)
MESH = pl.DeviceIdType.MESH


def twiddle_tables():
    n = np.arange(SUB, dtype=np.int64)[:, None]
    k2 = np.arange(CHANNELS // RADIX, dtype=np.int64)[None, :]
    scale = 1.0 / math.sqrt(NFFT)
    tables = np.zeros((4, 2 * SUB, 256), np.float64)
    for pair in range(4):
        for which in range(2):
            residue = RESIDUES[2 * pair + which]
            channel = FIRST_CH + RADIX * k2 + residue
            angle = ((n * channel) % NFFT) * (2.0 * math.pi / NFFT)
            cos, sin = np.cos(angle) * scale, np.sin(angle) * scale
            re, im = slice(which * 64, which * 64 + 64), slice(128 + which * 64, 192 + which * 64)
            if pair == 0:
                rows = slice(which * SUB, (which + 1) * SUB)
                tables[pair, rows, re] = cos
                tables[pair, rows, im] = -sin
            else:
                sign = 1.0 if which == 0 else -1.0
                tables[pair, :SUB, re] = cos
                tables[pair, SUB:, re] = -sign * sin
                tables[pair, :SUB, im] = -sin
                tables[pair, SUB:, im] = -sign * cos
    return tables.astype(jnp.bfloat16)


def al(x):
    return pl.multiple_of(x, 128)


def kernel(
    samples, fir, tables, group_row, pairs, out,
    volts, xs, wt, perm, fbuf, planes, spec, send, rows, cols, acc, stage,
    x_sem, w_sem, o_sem, own_sem, a2a_s, a2a_r, dir_s, dir_r, fwd_s, fwd_r, sib_s, sib_r,
):
    grp, tri = lax.axis_index("grp"), lax.axis_index("tri")
    gy, gz = grp // 4, lax.rem(grp, 4)
    cx, core = tri // 2, lax.rem(tri, 2)
    slots = pairs.shape[1]

    def group_at(dy, dz):
        return lax.rem(gy + dy, 4) * 4 + lax.rem(gz + dz, 4)

    def tri_at(dx):
        return lax.rem(cx + dx, 4) * 2 + core

    partners = [group_at(dy, dz) for dy in range(4) for dz in range(4) if (dy, dz) != (0, 0)]
    right, left, across = tri_at(1), tri_at(3), tri_at(2)
    sibling = cx * 2 + (1 - core)

    def frames_copy(i, count):
        src = pl.ds(al(i * (FSTEP * NFFT)), count * NFFT)
        dst = pl.ds(al(lax.rem(i, RING) * (FSTEP * NFFT)), count * NFFT)
        return pltpu.make_async_copy(samples.at[:, src], xs.at[:, dst], x_sem.at[i])

    for i in range(3):
        frames_copy(i, FSTEP).start()
    table_copy = pltpu.make_async_copy(tables, wt, w_sem)
    table_copy.start()

    barrier = pltpu.get_barrier_semaphore()
    for p in partners:
        pl.semaphore_signal(barrier, inc=1, device_id=(p, tri), device_id_type=MESH)
    for t in (right, left, sibling):
        pl.semaphore_signal(barrier, inc=1, device_id=(grp, t), device_id_type=MESH)

    number = lax.broadcasted_iota(jnp.int32, (64, CHANNELS), 1)
    for piece in range(RADIX):
        channel = lax.broadcasted_iota(jnp.int32, (64, CHANNELS), 0) * RADIX + RESIDUES[piece]
        groups = jnp.broadcast_to(group_row[...], (64, CHANNELS))
        mine = jnp.sum(jnp.where(number == channel, groups, 0), axis=1, keepdims=True)
        before = jnp.where((groups == mine) & (number < channel), 1, 0)
        rank = jnp.sum(before, axis=1, keepdims=True)
        one = jnp.where(number == mine * CH_GRP + rank, 1.0, 0.0)
        perm[pl.ds(piece * 64, 64), :] = one.astype(jnp.bfloat16)

    def a2a_copy(j, i):
        p = partners[i]
        return pltpu.make_async_remote_copy(
            src_ref=send.at[j, p], dst_ref=volts.at[j, tri, grp],
            send_sem=a2a_s.at[j], recv_sem=a2a_r.at[j],
            device_id=(p, tri), device_id_type=MESH)

    def own_copy(j):
        return pltpu.make_async_copy(send.at[j, grp], volts.at[j, tri, grp], own_sem.at[j])

    def part_copy(j, t, half, to, ssem, rsem):
        ref = volts.at[j, t] if half is None else volts.at[j, t, pl.ds(half * 8, 8)]
        return pltpu.make_async_remote_copy(
            src_ref=ref, dst_ref=ref, send_sem=ssem, recv_sem=rsem,
            device_id=(grp, to), device_id_type=MESH)

    def direct(j, way):
        return part_copy(j, tri, None, (right, left)[way], dir_s.at[way, j], dir_r.at[way, j])

    def forward(j, way):
        return part_copy(j, (left, right)[way], way, (right, left)[way], fwd_s.at[way, j], fwd_r.at[way, j])

    def share(j, which):
        return part_copy(j, (tri, left, right, across)[which], None, sibling, sib_s.at[which, j], sib_r.at[which, j])

    def stage_direct(j):
        own_copy(j).wait()
        some = volts.at[j, tri, pl.ds(0, GROUPS - 1)]
        pltpu.make_async_copy(some, some, a2a_r.at[j]).wait()
        for way in range(2):
            direct(j, way).start()
        share(j, 0).start()

    def stage_forward(j):
        for way in range(2):
            direct(j, way).wait_recv()
            forward(j, way).start()
        share(j, 1).start()
        share(j, 2).start()

    def stage_across(j):
        for way in range(2):
            forward(j, way).wait_recv()
        share(j, 3).start()

    half_root = math.sqrt(0.5)
    lane = lax.broadcasted_iota(jnp.int32, (DISH, 128), 1)

    def filter_tile(j, i):
        base = [lax.rem(j + k, RING) * (FSTEP * NFFT) for k in range(3)]
        for n1 in range(RADIX):
            off = n1 * SUB + i * 128
            coef = [fir[pl.ds(t, 1), pl.ds(al(off), 128)] for t in range(TAPS)]
            accs = [None] * FSTEP
            for fr in range(FSTEP + TAPS - 1):
                at = al(base[fr // FSTEP] + (fr % FSTEP) * NFFT + off)
                x = xs[:, pl.ds(at, 128)].astype(jnp.float32)
                for f in range(max(0, fr - TAPS + 1), min(FSTEP - 1, fr) + 1):
                    term = x * coef[fr - f]
                    accs[f] = term if accs[f] is None else accs[f] + term
                    if fr - f == TAPS - 1:
                        fbuf[n1, pl.ds(f * DISH, DISH), :] = accs[f]
        for f in range(FSTEP):
            at = pl.ds(f * DISH, DISH)
            v = [fbuf[n1, at, :] for n1 in range(RADIX)]
            a = [v[k] + v[k + 4] for k in range(4)]
            b = [v[k] - v[k + 4] for k in range(4)]
            even, odd = a[0] + a[2], a[1] + a[3]
            diff = (b[1] - b[3]) * half_root
            total = (b[1] + b[3]) * half_root
            res = (even + odd, even - odd, b[0] + diff, b[2] + total,
                   a[0] - a[2], a[1] - a[3], b[0] - diff, total - b[2])
            for k in range(RADIX):
                planes[at, pl.ds(al(k * SUB + i * 128), 128)] = res[k].astype(jnp.bfloat16)

    def transform(j):
        for p in range(4):
            got = jnp.dot(planes[:, p * 2048 : (p + 1) * 2048], wt[p], preferred_element_type=jnp.float32)
            got = got.astype(jnp.bfloat16)
            for part in range(2):
                spec[part * MROWS : (part + 1) * MROWS, p * 128 : (p + 1) * 128] = got[:, part * 128 : (part + 1) * 128]
        for two in range(2):
            sorted_ = jnp.dot(spec[...], perm[:, two * 256 : (two + 1) * 256], preferred_element_type=jnp.float32)
            for one in range(2):
                blk = sorted_[:, one * 128 : (one + 1) * 128]
                re = [blk[f * DISH : (f + 1) * DISH] for f in range(FSTEP)]
                im = [blk[MROWS + f * DISH : MROWS + (f + 1) * DISH] for f in range(FSTEP)]
                for hi in range(2):
                    if hi:
                        t = [jnp.where(lane < 64, pltpu.roll(r, 64, 1), m) for r, m in zip(re, im)]
                    else:
                        t = [jnp.where(lane < 64, r, pltpu.roll(m, 64, 1)) for r, m in zip(re, im)]
                    for bit in range(3):
                        hop = 1 << bit
                        odd = (lane >> (3 + bit)) & 1 == 1
                        new = list(t)
                        for k in range(FSTEP):
                            if not k & hop:
                                up = pltpu.roll(t[k + hop], 8 * hop, 1)
                                down = pltpu.roll(t[k], 128 - 8 * hop, 1)
                                new[k] = jnp.where(odd, up, t[k])
                                new[k + hop] = jnp.where(odd, t[k + hop], down)
                        t = new
                    for k in range(FSTEP):
                        send[j, two * 8 + one * 4 + hi * 2 + k // 4, k % 4] = t[k].astype(jnp.bfloat16)

    def correlate(k):
        for j in (2 * k, 2 * k + 1):
            for which in range(4):
                share(j, which).wait_recv()

        def row(o, carry):
            def arrange(b, c):
                for h in range(2):
                    v = volts[2 * k + h, :, b, o].reshape(BLOCK, 128)
                    rows[b, :, h * 128 : (h + 1) * 128] = v
                    vt = v.T
                    cols[b, h * 128 : (h + 1) * 128, 0:128] = vt
                    cols[b, h * 128 : h * 128 + 64, 128:256] = -vt[64:]
                    cols[b, h * 128 + 64 : (h + 1) * 128, 128:256] = vt[:64]
                return c

            lax.fori_loop(0, NBLK, arrange, 0, unroll=4)
            for s in range(slots):
                got = jnp.dot(rows[pairs[0, s]], cols[pairs[1, s]], preferred_element_type=jnp.float32)
                if k > 0:
                    got = got + acc[o, s]
                if k < CHUNKS // 2 - 1:
                    acc[o, s] = got
                else:
                    got = (got * (1.0 / (SPECTRA * FAVG))).astype(jnp.bfloat16)
                    for part in range(2):
                        stage[o, s, part] = got[:, part * 128 : (part + 1) * 128]
            if k == CHUNKS // 2 - 1:
                pltpu.make_async_copy(stage.at[o], out.at[o], o_sem.at[o]).start()
            return carry

        lax.fori_loop(0, ROWS, row, 0)

    def tiles(s, lo, hi):
        def tile(i, c):
            filter_tile(s, i)
            return c

        lax.fori_loop(lo, hi, tile, 0)

    def ship(s):
        transform(s)
        for i in range(GROUPS - 1):
            a2a_copy(s, i).start()
        own_copy(s).start()

    frames_copy(3, FSTEP).start()
    for i in range(3):
        frames_copy(i, FSTEP).wait()
    tiles(0, 0, SUB // 128)
    pl.semaphore_wait(barrier, len(partners) + 3)
    table_copy.wait()
    ship(0)

    def step(s, carry):
        @pl.when(s + 3 < CHUNKS + 1)
        def _():
            frames_copy(s + 3, FSTEP).start()

        @pl.when(s + 3 == CHUNKS + 1)
        def _():
            frames_copy(CHUNKS + 1, FSTEP - 1).start()

        @pl.when(s + 2 < CHUNKS + 1)
        def _():
            frames_copy(s + 2, FSTEP).wait()

        @pl.when(s + 2 == CHUNKS + 1)
        def _():
            frames_copy(CHUNKS + 1, FSTEP - 1).wait()

        tiles(s, 0, 5)
        stage_direct(s - 1)
        tiles(s, 5, SUB // 128)

        @pl.when(s >= 2)
        def _():
            stage_forward(s - 2)

        ship(s)

        @pl.when(s >= 3)
        def _():
            stage_across(s - 3)

        return carry

    lax.fori_loop(1, CHUNKS, step, 0)
    stage_direct(CHUNKS - 1)
    stage_forward(CHUNKS - 2)
    stage_across(CHUNKS - 3)
    correlate(0)
    stage_forward(CHUNKS - 1)
    stage_across(CHUNKS - 2)
    correlate(1)
    stage_across(CHUNKS - 1)
    correlate(2)
    correlate(3)

    def finish(j, carry):
        some = send.at[j, pl.ds(0, GROUPS - 1)]
        pltpu.make_async_copy(some, some, a2a_s.at[j]).wait()
        for way in range(2):
            direct(j, way).wait_send()
            forward(j, way).wait_send()
        for which in range(4):
            share(j, which).wait_send()
        return carry

    lax.fori_loop(0, CHUNKS, finish, 0)
    for o in range(ROWS):
        pltpu.make_async_copy(stage.at[o], out.at[o], o_sem.at[o]).wait()


def shards(samples, fir_taps, channel_group, tile_pairs):
    slots = tile_pairs.shape[1]
    tables = jnp.asarray(twiddle_tables())
    dma = pltpu.SemaphoreType.DMA
    any_spec = pl.BlockSpec(memory_space=pl.ANY)
    vmem = pl.BlockSpec(memory_space=pltpu.VMEM)
    smem = pl.BlockSpec(memory_space=pltpu.SMEM)
    return pl.pallas_call(
        kernel,
        out_shape=jax.ShapeDtypeStruct((ROWS, slots, 2, BLOCK, BLOCK), jnp.bfloat16),
        in_specs=[any_spec, vmem, any_spec, vmem, smem],
        out_specs=any_spec,
        scratch_shapes=[
            pltpu.VMEM((CHUNKS, TRI, NBLK, ROWS, DISH, 128), jnp.bfloat16),
            pltpu.VMEM((DISH, RING * FSTEP * NFFT), jnp.bfloat16),
            pltpu.VMEM(tables.shape, jnp.bfloat16),
            pltpu.VMEM((CHANNELS, CHANNELS), jnp.bfloat16),
            pltpu.VMEM((RADIX, MROWS, 128), jnp.float32),
            pltpu.VMEM((MROWS, NFFT), jnp.bfloat16),
            pltpu.VMEM((2 * MROWS, CHANNELS), jnp.bfloat16),
            pltpu.VMEM((CHUNKS, GROUPS, ROWS, DISH, 128), jnp.bfloat16),
            pltpu.VMEM((NBLK, BLOCK, 256), jnp.bfloat16),
            pltpu.VMEM((NBLK, 256, 256), jnp.bfloat16),
            pltpu.VMEM((ROWS, slots, BLOCK, 256), jnp.float32),
            pltpu.VMEM((ROWS, slots, 2, BLOCK, BLOCK), jnp.bfloat16),
            dma((CHUNKS + 2,)), dma, dma((ROWS,)), dma((CHUNKS,)), dma((CHUNKS,)), dma((CHUNKS,)),
            dma((2, CHUNKS)), dma((2, CHUNKS)), dma((2, CHUNKS)), dma((2, CHUNKS)),
            dma((4, CHUNKS)), dma((4, CHUNKS)),
        ],
        compiler_params=pltpu.CompilerParams(
            collective_id=0, has_side_effects=True, vmem_limit_bytes=58 << 20),
        name="correlator",
    )(samples, fir_taps, tables, channel_group.reshape(1, CHANNELS), tile_pairs)


def solution(mesh):
    in_specs = (P(("grp", "tri"), None), P(), P(), P(None, "tri"))
    out_specs = P("grp", "tri", None, None, None)
    return jax.shard_map(shards, mesh=mesh, in_specs=in_specs, out_specs=out_specs, check_vma=False)
```

```python
import math

import jax
import jax.numpy as jnp
import numpy as np
from jax import lax
from jax.experimental import pallas as pl
from jax.experimental.pallas import tpu as pltpu
from jax.sharding import PartitionSpec as P

NFFT = 8192
TAPS = 16
BLOCK = 128
FIRST_CH = 1024
CHANNELS = 512
CH_GRP = 32
FAVG = 8
SPECTRA = 64
NBLK = 16
DISH = 16
GROUPS = 16
TRI = 8
ROWS = CH_GRP // FAVG
FSTEP = 8
CHUNKS = SPECTRA // FSTEP
MROWS = FSTEP * DISH
FAR = (range(0, 8), range(8, 17))
PIECES = ((0, 2, 4, 8), (8, 10, 13, 17))
RING = 4
RADIX = 8
SUB = NFFT // RADIX
RESIDUES = (0, 4, 1, 7, 2, 6, 3, 5)
MESH = pl.DeviceIdType.MESH


def twiddle_tables():
    n = np.arange(SUB, dtype=np.int64)[:, None]
    k2 = np.arange(CHANNELS // RADIX, dtype=np.int64)[None, :]
    scale = 1.0 / math.sqrt(NFFT)
    tables = np.zeros((4, 2 * SUB, 256), np.float64)
    for pair in range(4):
        for which in range(2):
            residue = RESIDUES[2 * pair + which]
            channel = FIRST_CH + RADIX * k2 + residue
            angle = ((n * channel) % NFFT) * (2.0 * math.pi / NFFT)
            cos, sin = np.cos(angle) * scale, np.sin(angle) * scale
            re, im = slice(which * 64, which * 64 + 64), slice(128 + which * 64, 192 + which * 64)
            if pair == 0:
                rows = slice(which * SUB, (which + 1) * SUB)
                tables[pair, rows, re] = cos
                tables[pair, rows, im] = -sin
            else:
                sign = 1.0 if which == 0 else -1.0
                tables[pair, :SUB, re] = cos
                tables[pair, SUB:, re] = -sign * sin
                tables[pair, :SUB, im] = -sin
                tables[pair, SUB:, im] = -sign * cos
    return tables.astype(jnp.bfloat16)


def al(x):
    return pl.multiple_of(x, 128)


def kernel(
    samples, fir, tables, group_row, pairs, own_pairs, out,
    volts, mine4, pairs_in, near_pairs, xs, wt, perm, fbuf, planes, spec, send, rows, cols, acc, stage,
    x_sem, w_sem, o_s, o_r, p_s, p_r, p_l, own_sem, a2a_s, a2a_r, dir_s, dir_r, fwd_s, fwd_r, sib_s, sib_r,
):
    grp, tri = lax.axis_index("grp"), lax.axis_index("tri")
    gy, gz = grp // 4, lax.rem(grp, 4)
    cx, core = tri // 2, lax.rem(tri, 2)
    slots = own_pairs.shape[1]
    last = CHUNKS // 2 - 1

    def group_at(dy, dz):
        return lax.rem(gy + dy, 4) * 4 + lax.rem(gz + dz, 4)

    def tri_at(dx):
        return lax.rem(cx + dx, 4) * 2 + core

    partners = [group_at(dy, dz) for dy in range(4) for dz in range(4) if (dy, dz) != (0, 0)]
    right, left, across = tri_at(1), tri_at(3), tri_at(2)
    sibling = cx * 2 + (1 - core)

    def frames_copy(i, count):
        src = pl.ds(al(i * (FSTEP * NFFT)), count * NFFT)
        dst = pl.ds(al(lax.rem(i, RING) * (FSTEP * NFFT)), count * NFFT)
        return pltpu.make_async_copy(samples.at[:, src], xs.at[:, dst], x_sem.at[i])

    for i in range(3):
        frames_copy(i, FSTEP).start()
    table_copy = pltpu.make_async_copy(tables, wt, w_sem)
    table_copy.start()

    barrier = pltpu.get_barrier_semaphore()
    for p in partners:
        pl.semaphore_signal(barrier, inc=1, device_id=(p, tri), device_id_type=MESH)
    for t in (right, left, sibling):
        pl.semaphore_signal(barrier, inc=1, device_id=(grp, t), device_id_type=MESH)

    number = lax.broadcasted_iota(jnp.int32, (64, CHANNELS), 1)
    for piece in range(RADIX):
        channel = lax.broadcasted_iota(jnp.int32, (64, CHANNELS), 0) * RADIX + RESIDUES[piece]
        groups = jnp.broadcast_to(group_row[...], (64, CHANNELS))
        mine = jnp.sum(jnp.where(number == channel, groups, 0), axis=1, keepdims=True)
        before = jnp.where((groups == mine) & (number < channel), 1, 0)
        rank = jnp.sum(before, axis=1, keepdims=True)
        one = jnp.where(number == mine * CH_GRP + rank, 1.0, 0.0)
        perm[pl.ds(piece * 64, 64), :] = one.astype(jnp.bfloat16)

    def a2a_copy(j, i):
        p = partners[i]
        return pltpu.make_async_remote_copy(
            src_ref=send.at[j, p], dst_ref=mine4.at[j, :, grp],
            send_sem=a2a_s.at[j], recv_sem=a2a_r.at[j],
            device_id=(p, tri), device_id_type=MESH)

    def own_copy(j):
        return pltpu.make_async_copy(send.at[j, grp], mine4.at[j, :, grp], own_sem.at[0, j])

    def keep_copy(j):
        return pltpu.make_async_copy(mine4.at[j, pl.ds(1, 3)], volts.at[j, tri], own_sem.at[1, j])

    def remote(src, dst, to, ssem, rsem):
        return pltpu.make_async_remote_copy(
            src_ref=src, dst_ref=dst, send_sem=ssem, recv_sem=rsem,
            device_id=(grp, to), device_id_type=MESH)

    def direct(j, part):
        if part == 0:
            src, dst, way = mine4.at[j, pl.ds(2, 2)], volts.at[j, tri, pl.ds(0, 2)], 0
        elif part == 1:
            src, dst, way = mine4.at[j, 0], volts.at[j, tri, 2], 0
        else:
            src, dst, way = mine4.at[j, pl.ds(0, 3)], volts.at[j, tri], 1
        return remote(src, dst, (right, left)[way], dir_s.at[part, j], dir_r.at[part, j])

    def forward(j, way, whole):
        t = (left, right)[way]
        if whole:
            src, dst = volts.at[j, t, 1], volts.at[j, t, 2 * way]
        else:
            half = pl.ds(8 * way, 8)
            src, dst = volts.at[j, t, 2 - 2 * way, half], volts.at[j, t, 1, half]
        return remote(src, dst, (right, left)[way], fwd_s.at[way, whole, j], fwd_r.at[way, whole, j])

    def share(j, which):
        t = (tri, left, right, across)[which]
        src = mine4.at[j, pl.ds(1, 3)] if which == 0 else volts.at[j, t]
        return remote(src, volts.at[j, t], sibling, sib_s.at[which, j], sib_r.at[which, j])

    def stage_direct(j):
        own_copy(j).wait()
        some = mine4.at[j, :, pl.ds(0, GROUPS - 1)]
        pltpu.make_async_copy(some, some, a2a_r.at[j]).wait()
        for part in (2, 0, 1):
            direct(j, part).start()
        share(j, 0).start()
        keep_copy(j).start()

    def stage_forward(j):
        direct(j, 2).wait_recv()
        for whole in (1, 0):
            forward(j, 1, whole).start()
        direct(j, 0).wait_recv()
        direct(j, 1).wait_recv()
        for whole in (1, 0):
            forward(j, 0, whole).start()
        share(j, 1).start()
        share(j, 2).start()

    def stage_across(j):
        for way in range(2):
            for whole in range(2):
                forward(j, way, whole).wait_recv()
        share(j, 3).start()

    half_root = math.sqrt(0.5)
    lane = lax.broadcasted_iota(jnp.int32, (DISH, 128), 1)

    def filter_tile(j, i):
        base = [lax.rem(j + k, RING) * (FSTEP * NFFT) for k in range(3)]
        for n1 in range(RADIX):
            off = n1 * SUB + i * 128
            coef = [fir[pl.ds(t, 1), pl.ds(al(off), 128)] for t in range(TAPS)]
            accs = [None] * FSTEP
            for fr in range(FSTEP + TAPS - 1):
                at = al(base[fr // FSTEP] + (fr % FSTEP) * NFFT + off)
                x = xs[:, pl.ds(at, 128)].astype(jnp.float32)
                for f in range(max(0, fr - TAPS + 1), min(FSTEP - 1, fr) + 1):
                    term = x * coef[fr - f]
                    accs[f] = term if accs[f] is None else accs[f] + term
                    if fr - f == TAPS - 1:
                        fbuf[n1, pl.ds(f * DISH, DISH), :] = accs[f]
        for f in range(FSTEP):
            at = pl.ds(f * DISH, DISH)
            v = [fbuf[n1, at, :] for n1 in range(RADIX)]
            a = [v[k] + v[k + 4] for k in range(4)]
            b = [v[k] - v[k + 4] for k in range(4)]
            even, odd = a[0] + a[2], a[1] + a[3]
            diff = (b[1] - b[3]) * half_root
            total = (b[1] + b[3]) * half_root
            res = (even + odd, even - odd, b[0] + diff, b[2] + total,
                   a[0] - a[2], a[1] - a[3], b[0] - diff, total - b[2])
            for k in range(RADIX):
                planes[at, pl.ds(al(k * SUB + i * 128), 128)] = res[k].astype(jnp.bfloat16)

    def transform(j):
        for p in range(4):
            got = jnp.dot(planes[:, p * 2048 : (p + 1) * 2048], wt[p], preferred_element_type=jnp.float32)
            got = got.astype(jnp.bfloat16)
            for part in range(2):
                spec[part * MROWS : (part + 1) * MROWS, p * 128 : (p + 1) * 128] = got[:, part * 128 : (part + 1) * 128]
        for two in range(2):
            sorted_ = jnp.dot(spec[...], perm[:, two * 256 : (two + 1) * 256], preferred_element_type=jnp.float32)
            for one in range(2):
                blk = sorted_[:, one * 128 : (one + 1) * 128]
                re = [blk[f * DISH : (f + 1) * DISH] for f in range(FSTEP)]
                im = [blk[MROWS + f * DISH : MROWS + (f + 1) * DISH] for f in range(FSTEP)]
                for hi in range(2):
                    if hi:
                        t = [jnp.where(lane < 64, pltpu.roll(r, 64, 1), m) for r, m in zip(re, im)]
                    else:
                        t = [jnp.where(lane < 64, r, pltpu.roll(m, 64, 1)) for r, m in zip(re, im)]
                    for bit in range(3):
                        hop = 1 << bit
                        odd = (lane >> (3 + bit)) & 1 == 1
                        new = list(t)
                        for k in range(FSTEP):
                            if not k & hop:
                                up = pltpu.roll(t[k + hop], 8 * hop, 1)
                                down = pltpu.roll(t[k], 128 - 8 * hop, 1)
                                new[k] = jnp.where(odd, up, t[k])
                                new[k + hop] = jnp.where(odd, t[k + hop], down)
                        t = new
                    for k in range(FSTEP):
                        send[j, two * 8 + one * 4 + hi * 2 + k // 4, lax.rem(k % 4 + 6 - cx, 4)] = t[k].astype(jnp.bfloat16)

    def arrived(k):
        for j in (2 * k, 2 * k + 1):
            keep_copy(j).wait()
            for which in range(4):
                share(j, which).wait_recv()

    def arrange(k, r, slot):
        def block(b, c):
            for h in range(2):
                v = volts[2 * k + h, :, r, b].reshape(BLOCK, 128)
                rows[slot, b, :, h * 128 : (h + 1) * 128] = v
                vt = v.T
                cols[slot, b, h * 128 : (h + 1) * 128, 0:128] = vt
                cols[slot, b, h * 128 : h * 128 + 64, 128:256] = -vt[64:]
                cols[slot, b, h * 128 + 64 : (h + 1) * 128, 128:256] = vt[:64]
            return c

        lax.fori_loop(0, NBLK, block, 0, unroll=4)

    def product(slot, ref, s):
        return jnp.dot(rows[slot, ref[0, s]], cols[slot, ref[1, s]], preferred_element_type=jnp.float32)

    def correlate(k):
        arrived(k)

        def add(r, slot, ref, s):
            got = product(slot, ref, s)
            acc[r, s] = got if k == 0 else got + acc[r, s]

        for r, slot in ((0, 0), (2, 1), (1, 0)):
            arrange(k, r, slot)
            for s in range(slots):
                add(r, slot, own_pairs, s)
            if r != 1:
                for s in FAR[slot]:
                    add(3, slot, near_pairs.at[slot], s)

    def result(r, slot, ref, s):
        got = (product(slot, ref, s) + acc[r, s]) * (1.0 / (SPECTRA * FAVG))
        return got.astype(jnp.bfloat16)

    def deliver(slot, piece):
        lo, hi = PIECES[slot][piece], PIECES[slot][piece + 1]
        part = pl.ds(lo, hi - lo)
        return remote(stage.at[part], out.at[lax.rem(cx + 3 + 2 * slot, 4), part], (right, left)[slot],
                      o_s.at[slot, piece], o_r.at[slot, piece])

    def final():
        arrived(last)
        for slot in range(2):
            arrange(last, 2 * slot, slot)
            for piece in range(len(PIECES[slot]) - 1):
                for s in range(PIECES[slot][piece], PIECES[slot][piece + 1]):
                    got = result(3, slot, near_pairs.at[slot], s)
                    for part in range(2):
                        stage[s, part] = got[:, part * 128 : (part + 1) * 128]
                deliver(slot, piece).start()
        for r, slot in ((0, 0), (2, 1), (1, 0)):
            if r == 1:
                arrange(last, r, slot)
            row = lax.rem(cx + 3 + r, 4)
            for s in range(slots):
                got = result(r, slot, own_pairs, s)
                for part in range(2):
                    out[row, s, part] = got[:, part * 128 : (part + 1) * 128]

    def pairs_copy(way):
        return remote(pairs, pairs_in.at[way], (left, right)[way], p_s.at[way], p_r.at[way])

    def tiles(s, lo, hi):
        def tile(i, c):
            filter_tile(s, i)
            return c

        lax.fori_loop(lo, hi, tile, 0)

    def ship(s):
        transform(s)
        for i in range(GROUPS - 1):
            a2a_copy(s, i).start()
        own_copy(s).start()

    frames_copy(3, FSTEP).start()
    for i in range(3):
        frames_copy(i, FSTEP).wait()
    tiles(0, 0, SUB // 128)
    pl.semaphore_wait(barrier, len(partners) + 3)
    table_copy.wait()
    for way in range(2):
        pairs_copy(way).start()
    ship(0)

    def step(s, carry):
        @pl.when(s + 3 < CHUNKS + 1)
        def _():
            frames_copy(s + 3, FSTEP).start()

        @pl.when(s + 3 == CHUNKS + 1)
        def _():
            frames_copy(CHUNKS + 1, FSTEP - 1).start()

        @pl.when(s + 2 < CHUNKS + 1)
        def _():
            frames_copy(s + 2, FSTEP).wait()

        @pl.when(s + 2 == CHUNKS + 1)
        def _():
            frames_copy(CHUNKS + 1, FSTEP - 1).wait()

        tiles(s, 0, SUB // 128)
        stage_direct(s - 1)

        @pl.when(s >= 2)
        def _():
            stage_forward(s - 2)

        @pl.when(s >= 3)
        def _():
            stage_across(s - 3)

        ship(s)
        return carry

    lax.fori_loop(1, CHUNKS, step, 0)
    for way in range(2):
        pairs_copy(way).wait()
        pltpu.make_async_copy(pairs_in.at[way], near_pairs.at[way], p_l.at[way]).start()
    for way in range(2):
        pltpu.make_async_copy(pairs_in.at[way], near_pairs.at[way], p_l.at[way]).wait()
    correlate(0)
    stage_forward(CHUNKS - 2)
    stage_across(CHUNKS - 3)
    stage_direct(CHUNKS - 1)
    correlate(1)
    stage_forward(CHUNKS - 1)
    stage_across(CHUNKS - 2)
    correlate(2)
    stage_across(CHUNKS - 1)
    final()

    def finish(j, carry):
        some = send.at[j, pl.ds(0, GROUPS - 1)]
        pltpu.make_async_copy(some, some, a2a_s.at[j]).wait()
        for part in range(3):
            direct(j, part).wait_send()
        for way in range(2):
            for whole in range(2):
                forward(j, way, whole).wait_send()
        for which in range(4):
            share(j, which).wait_send()
        return carry

    lax.fori_loop(0, CHUNKS, finish, 0)
    for slot in range(2):
        for piece in range(len(PIECES[slot]) - 1):
            deliver(slot, piece).wait_send()
            deliver(slot, piece).wait_recv()


def shards(samples, fir_taps, channel_group, tile_pairs):
    slots = tile_pairs.shape[1]
    pieces = len(PIECES[0]) - 1
    tables = jnp.asarray(twiddle_tables())
    dma = pltpu.SemaphoreType.DMA
    any_spec = pl.BlockSpec(memory_space=pl.ANY)
    vmem = pl.BlockSpec(memory_space=pltpu.VMEM)
    smem = pl.BlockSpec(memory_space=pltpu.SMEM)
    return pl.pallas_call(
        kernel,
        out_shape=pltpu.VMEM((ROWS, slots, 2, BLOCK, BLOCK), jnp.bfloat16),
        in_specs=[any_spec, vmem, any_spec, vmem, any_spec, smem],
        out_specs=vmem,
        scratch_shapes=[
            pltpu.VMEM((CHUNKS, TRI, 3, NBLK, DISH, 128), jnp.bfloat16),
            pltpu.VMEM((CHUNKS, ROWS, NBLK, DISH, 128), jnp.bfloat16),
            pltpu.VMEM((2, 2, slots), jnp.int32),
            pltpu.SMEM((2, 2, slots), jnp.int32),
            pltpu.VMEM((DISH, RING * FSTEP * NFFT), jnp.bfloat16),
            pltpu.VMEM(tables.shape, jnp.bfloat16),
            pltpu.VMEM((CHANNELS, CHANNELS), jnp.bfloat16),
            pltpu.VMEM((RADIX, MROWS, 128), jnp.float32),
            pltpu.VMEM((MROWS, NFFT), jnp.bfloat16),
            pltpu.VMEM((2 * MROWS, CHANNELS), jnp.bfloat16),
            pltpu.VMEM((CHUNKS, GROUPS, ROWS, DISH, 128), jnp.bfloat16),
            pltpu.VMEM((2, NBLK, BLOCK, 256), jnp.bfloat16),
            pltpu.VMEM((2, NBLK, 256, 256), jnp.bfloat16),
            pltpu.VMEM((4, slots, BLOCK, 256), jnp.float32),
            pltpu.VMEM((slots, 2, BLOCK, BLOCK), jnp.bfloat16),
            dma((CHUNKS + 2,)), dma, dma((2, pieces)), dma((2, pieces)), dma((2,)), dma((2,)), dma((2,)),
            dma((2, CHUNKS)), dma((CHUNKS,)), dma((CHUNKS,)),
            dma((3, CHUNKS)), dma((3, CHUNKS)), dma((2, 2, CHUNKS)), dma((2, 2, CHUNKS)),
            dma((4, CHUNKS)), dma((4, CHUNKS)),
        ],
        compiler_params=pltpu.CompilerParams(
            collective_id=0, has_side_effects=True, vmem_limit_bytes=56 << 20),
        name="correlator",
    )(samples, fir_taps, tables, channel_group.reshape(1, CHANNELS), tile_pairs, tile_pairs)


def solution(mesh):
    in_specs = (P(("grp", "tri"), None), P(), P(), P(None, "tri"))
    out_specs = P("grp", "tri", None, None, None)
    return jax.shard_map(shards, mesh=mesh, in_specs=in_specs, out_specs=out_specs, check_vma=False)
```

```python
import math

import jax
import jax.numpy as jnp
import numpy as np
from jax import lax
from jax.experimental import pallas as pl
from jax.experimental.pallas import tpu as pltpu
from jax.sharding import PartitionSpec as P

NFFT = 8192
TAPS = 16
BLOCK = 128
FIRST_CH = 1024
CHANNELS = 512
CH_GRP = 32
FAVG = 8
SPECTRA = 64
NBLK = 16
DISH = 16
GROUPS = 16
TRI = 8
ROWS = CH_GRP // FAVG
FSTEP = 8
CHUNKS = SPECTRA // FSTEP
MROWS = FSTEP * DISH
FAR = (range(0, 9), range(9, 17))
PIECES = ((0, 2, 5, 9), (9, 11, 13, 17))
RING = 4
RADIX = 8
SUB = NFFT // RADIX
RESIDUES = (0, 4, 1, 7, 2, 6, 3, 5)
MESH = pl.DeviceIdType.MESH


def twiddle_tables():
    n = np.arange(SUB, dtype=np.int64)[:, None]
    k2 = np.arange(CHANNELS // RADIX, dtype=np.int64)[None, :]
    scale = 1.0 / math.sqrt(NFFT)
    tables = np.zeros((4, 2 * SUB, 256), np.float64)
    for pair in range(4):
        for which in range(2):
            residue = RESIDUES[2 * pair + which]
            channel = FIRST_CH + RADIX * k2 + residue
            angle = ((n * channel) % NFFT) * (2.0 * math.pi / NFFT)
            cos, sin = np.cos(angle) * scale, np.sin(angle) * scale
            re, im = slice(which * 64, which * 64 + 64), slice(128 + which * 64, 192 + which * 64)
            if pair == 0:
                rows = slice(which * SUB, (which + 1) * SUB)
                tables[pair, rows, re] = cos
                tables[pair, rows, im] = -sin
            else:
                sign = 1.0 if which == 0 else -1.0
                tables[pair, :SUB, re] = cos
                tables[pair, SUB:, re] = -sign * sin
                tables[pair, :SUB, im] = -sin
                tables[pair, SUB:, im] = -sign * cos
    return tables.astype(jnp.bfloat16)


def al(x):
    return pl.multiple_of(x, 128)


def kernel(
    samples, taps, tables, group_row, pairs, own_pairs, out,
    volts, mine4, pairs_in, near_pairs, xs, fir, wt, perm, fbuf, planes, spec, send, rows, cols, acc, stage,
    x_sem, w_sem, o_s, o_r, p_s, p_r, p_l, own_sem, a2a_s, a2a_r, dir_s, dir_r, fwd_s, fwd_r, sib_s, sib_r,
):
    grp, tri = lax.axis_index("grp"), lax.axis_index("tri")
    gy, gz = grp // 4, lax.rem(grp, 4)
    cx, core = tri // 2, lax.rem(tri, 2)
    slots = own_pairs.shape[1]
    last = CHUNKS // 2 - 1

    def group_at(dy, dz):
        return lax.rem(gy + dy, 4) * 4 + lax.rem(gz + dz, 4)

    def tri_at(dx):
        return lax.rem(cx + dx, 4) * 2 + core

    partners = [group_at(dy, dz) for dy in range(4) for dz in range(4) if (dy, dz) != (0, 0)]
    right, left, across = tri_at(1), tri_at(3), tri_at(2)
    sibling = cx * 2 + (1 - core)

    def frames_copy(i, count):
        src = pl.ds(al(i * (FSTEP * NFFT)), count * NFFT)
        dst = pl.ds(al(lax.rem(i, RING) * (FSTEP * NFFT)), count * NFFT)
        return pltpu.make_async_copy(samples.at[:, src], xs.at[:, dst], x_sem.at[i])

    table_copy = pltpu.make_async_copy(tables, wt, w_sem.at[0])
    taps_copy = pltpu.make_async_copy(taps, fir, w_sem.at[1])
    taps_copy.start()
    for i in range(3):
        frames_copy(i, FSTEP).start()

    barrier = pltpu.get_barrier_semaphore()
    for p in partners:
        pl.semaphore_signal(barrier, inc=1, device_id=(p, tri), device_id_type=MESH)
    for t in (right, left, sibling):
        pl.semaphore_signal(barrier, inc=1, device_id=(grp, t), device_id_type=MESH)

    number = lax.broadcasted_iota(jnp.int32, (64, CHANNELS), 1)
    for piece in range(RADIX):
        channel = lax.broadcasted_iota(jnp.int32, (64, CHANNELS), 0) * RADIX + RESIDUES[piece]
        groups = jnp.broadcast_to(group_row[...], (64, CHANNELS))
        mine = jnp.sum(jnp.where(number == channel, groups, 0), axis=1, keepdims=True)
        before = jnp.where((groups == mine) & (number < channel), 1, 0)
        rank = jnp.sum(before, axis=1, keepdims=True)
        one = jnp.where(number == mine * CH_GRP + rank, 1.0, 0.0)
        perm[pl.ds(piece * 64, 64), :] = one.astype(jnp.bfloat16)

    def a2a_copy(j, i):
        p = partners[i]
        return pltpu.make_async_remote_copy(
            src_ref=send.at[j, p], dst_ref=mine4.at[j, :, grp],
            send_sem=a2a_s.at[j], recv_sem=a2a_r.at[j],
            device_id=(p, tri), device_id_type=MESH)

    def own_copy(j):
        return pltpu.make_async_copy(send.at[j, grp], mine4.at[j, :, grp], own_sem.at[0, j])

    def keep_copy(j):
        return pltpu.make_async_copy(mine4.at[j, pl.ds(1, 3)], volts.at[j, tri], own_sem.at[1, j])

    def remote(src, dst, to, ssem, rsem):
        return pltpu.make_async_remote_copy(
            src_ref=src, dst_ref=dst, send_sem=ssem, recv_sem=rsem,
            device_id=(grp, to), device_id_type=MESH)

    def direct(j, part):
        if part == 0:
            src, dst, way = mine4.at[j, pl.ds(2, 2)], volts.at[j, tri, pl.ds(0, 2)], 0
        elif part == 1:
            src, dst, way = mine4.at[j, 0], volts.at[j, tri, 2], 0
        else:
            src, dst, way = mine4.at[j, pl.ds(0, 3)], volts.at[j, tri], 1
        return remote(src, dst, (right, left)[way], dir_s.at[part, j], dir_r.at[part, j])

    def forward(j, way, whole):
        t = (left, right)[way]
        if whole:
            src, dst = volts.at[j, t, 1], volts.at[j, t, 2 * way]
        else:
            half = pl.ds(8 * way, 8)
            src, dst = volts.at[j, t, 2 - 2 * way, half], volts.at[j, t, 1, half]
        return remote(src, dst, (right, left)[way], fwd_s.at[way, whole, j], fwd_r.at[way, whole, j])

    def share(j, which):
        t = (tri, left, right, across)[which]
        src = mine4.at[j, pl.ds(1, 3)] if which == 0 else volts.at[j, t]
        return remote(src, volts.at[j, t], sibling, sib_s.at[which, j], sib_r.at[which, j])

    def stage_direct(j):
        own_copy(j).wait()
        some = mine4.at[j, :, pl.ds(0, GROUPS - 1)]
        pltpu.make_async_copy(some, some, a2a_r.at[j]).wait()
        for part in (2, 0, 1):
            direct(j, part).start()
        share(j, 0).start()
        keep_copy(j).start()

    def stage_forward(j):
        direct(j, 2).wait_recv()
        for whole in (1, 0):
            forward(j, 1, whole).start()
        direct(j, 0).wait_recv()
        direct(j, 1).wait_recv()
        for whole in (1, 0):
            forward(j, 0, whole).start()
        share(j, 1).start()
        share(j, 2).start()

    def stage_across(j):
        for way in range(2):
            for whole in range(2):
                forward(j, way, whole).wait_recv()
        share(j, 3).start()

    half_root = math.sqrt(0.5)
    lane = lax.broadcasted_iota(jnp.int32, (DISH, 128), 1)

    def filter_tile(j, i):
        base = [lax.rem(j + k, RING) * (FSTEP * NFFT) for k in range(3)]
        for n1 in range(RADIX):
            off = n1 * SUB + i * 128
            coef = [fir[pl.ds(t, 1), pl.ds(al(off), 128)] for t in range(TAPS)]
            accs = [None] * FSTEP
            for fr in range(FSTEP + TAPS - 1):
                at = al(base[fr // FSTEP] + (fr % FSTEP) * NFFT + off)
                x = xs[:, pl.ds(at, 128)].astype(jnp.float32)
                for f in range(max(0, fr - TAPS + 1), min(FSTEP - 1, fr) + 1):
                    term = x * coef[fr - f]
                    accs[f] = term if accs[f] is None else accs[f] + term
                    if fr - f == TAPS - 1:
                        fbuf[n1, pl.ds(f * DISH, DISH), :] = accs[f]
        for f in range(FSTEP):
            at = pl.ds(f * DISH, DISH)
            v = [fbuf[n1, at, :] for n1 in range(RADIX)]
            a = [v[k] + v[k + 4] for k in range(4)]
            b = [v[k] - v[k + 4] for k in range(4)]
            even, odd = a[0] + a[2], a[1] + a[3]
            diff = (b[1] - b[3]) * half_root
            total = (b[1] + b[3]) * half_root
            res = (even + odd, even - odd, b[0] + diff, b[2] + total,
                   a[0] - a[2], a[1] - a[3], b[0] - diff, total - b[2])
            for k in range(RADIX):
                planes[at, pl.ds(al(k * SUB + i * 128), 128)] = res[k].astype(jnp.bfloat16)

    def transform(j):
        for p in range(4):
            got = jnp.dot(planes[:, p * 2048 : (p + 1) * 2048], wt[p], preferred_element_type=jnp.float32)
            got = got.astype(jnp.bfloat16)
            for part in range(2):
                spec[part * MROWS : (part + 1) * MROWS, p * 128 : (p + 1) * 128] = got[:, part * 128 : (part + 1) * 128]
        for two in range(2):
            sorted_ = jnp.dot(spec[...], perm[:, two * 256 : (two + 1) * 256], preferred_element_type=jnp.float32)
            for one in range(2):
                blk = sorted_[:, one * 128 : (one + 1) * 128]
                t = []
                for k in range(2 * FSTEP):
                    v = blk[k * DISH : (k + 1) * DISH]
                    t.append(pltpu.roll(v, 8 * k, 1) if k else v)
                for bit in range(4):
                    odd = (lane >> (3 + bit)) & 1 == 1
                    t = [jnp.where(odd, t[(k + (1 << bit)) % 16], t[k]) for k in range(16)]
                for go in range(16):
                    send[j, two * 8 + one * 4 + go // 4, lax.rem(go % 4 + 6 - cx, 4)] = t[-go % 16].astype(jnp.bfloat16)

    def arrived(k):
        for j in (2 * k, 2 * k + 1):
            keep_copy(j).wait()
            for which in range(4):
                share(j, which).wait_recv()

    def arrange(k, r, slot):
        go = lax.rem(grp, 4) * 4 + lax.rem(cx + 3 + r, 4)
        place = lax.rem((lax.broadcasted_iota(jnp.int32, (BLOCK, BLOCK), 0) >> 3) - go + 16, 16)
        sign = jnp.where(place < FSTEP, -1.0, 1.0).astype(jnp.bfloat16)

        def block(b, c):
            for h in range(2):
                v = volts[2 * k + h, :, r, b].reshape(BLOCK, 128)
                rows[slot, b, :, h * 128 : (h + 1) * 128] = v
                vt = v.T
                cols[slot, b, h * 128 : (h + 1) * 128, 0:128] = vt
                swapped = jnp.concatenate([vt[64:], vt[:64]], axis=0)
                cols[slot, b, h * 128 : (h + 1) * 128, 128:256] = swapped * sign
            return c

        lax.fori_loop(0, NBLK, block, 0, unroll=4)

    def product(slot, ref, s):
        return jnp.dot(rows[slot, ref[0, s]], cols[slot, ref[1, s]], preferred_element_type=jnp.float32)

    def correlate(k):
        arrived(k)

        def add(r, slot, ref, s):
            got = product(slot, ref, s)
            acc[r, s] = got if k == 0 else got + acc[r, s]

        for r, slot in ((0, 0), (2, 1), (1, 0)):
            arrange(k, r, slot)
            for s in range(slots):
                add(r, slot, own_pairs, s)
            if r != 1:
                for s in FAR[slot]:
                    add(3, slot, near_pairs.at[slot], s)

    def result(r, slot, ref, s):
        got = (product(slot, ref, s) + acc[r, s]) * (1.0 / (SPECTRA * FAVG))
        return got.astype(jnp.bfloat16)

    def deliver(slot, piece):
        lo, hi = PIECES[slot][piece], PIECES[slot][piece + 1]
        part = pl.ds(lo, hi - lo)
        return remote(stage.at[part], out.at[lax.rem(cx + 3 + 2 * slot, 4), part], (right, left)[slot],
                      o_s.at[slot, piece], o_r.at[slot, piece])

    def final():
        arrived(last)
        for slot in range(2):
            arrange(last, 2 * slot, slot)
            for piece in range(len(PIECES[slot]) - 1):
                for s in range(PIECES[slot][piece], PIECES[slot][piece + 1]):
                    got = result(3, slot, near_pairs.at[slot], s)
                    for part in range(2):
                        stage[s, part] = got[:, part * 128 : (part + 1) * 128]
                deliver(slot, piece).start()
        for r, slot in ((0, 0), (2, 1), (1, 0)):
            if r == 1:
                arrange(last, r, slot)
            row = lax.rem(cx + 3 + r, 4)
            for s in range(slots):
                got = result(r, slot, own_pairs, s)
                for part in range(2):
                    out[row, s, part] = got[:, part * 128 : (part + 1) * 128]

    def pairs_copy(way):
        return remote(pairs, pairs_in.at[way], (left, right)[way], p_s.at[way], p_r.at[way])

    def tiles(s, send_previous):
        def tile(i, c):
            filter_tile(s, i)
            return c

        lax.fori_loop(0, SUB // 128, tile, 0)

    def ship(s):
        transform(s)
        for i in range(GROUPS - 1):
            a2a_copy(s, i).start()
        own_copy(s).start()

    taps_copy.wait()
    for i in range(3):
        frames_copy(i, FSTEP).wait()
    table_copy.start()
    frames_copy(3, FSTEP).start()
    tiles(0, False)
    pl.semaphore_wait(barrier, len(partners) + 3)
    table_copy.wait()
    for way in range(2):
        pairs_copy(way).start()
    ship(0)

    def step(s, carry):
        @pl.when(s + 3 < CHUNKS + 1)
        def _():
            frames_copy(s + 3, FSTEP).start()

        @pl.when(s + 3 == CHUNKS + 1)
        def _():
            frames_copy(CHUNKS + 1, FSTEP - 1).start()

        @pl.when(s + 2 < CHUNKS + 1)
        def _():
            frames_copy(s + 2, FSTEP).wait()

        @pl.when(s + 2 == CHUNKS + 1)
        def _():
            frames_copy(CHUNKS + 1, FSTEP - 1).wait()

        tiles(s, True)
        stage_direct(s - 1)

        ship(s)

        @pl.when(s >= 2)
        def _():
            stage_forward(s - 2)

        @pl.when(s >= 3)
        def _():
            stage_across(s - 3)

        return carry

    lax.fori_loop(1, CHUNKS, step, 0)
    for way in range(2):
        pairs_copy(way).wait()
        pltpu.make_async_copy(pairs_in.at[way], near_pairs.at[way], p_l.at[way]).start()
    for way in range(2):
        pltpu.make_async_copy(pairs_in.at[way], near_pairs.at[way], p_l.at[way]).wait()
    correlate(0)
    stage_forward(CHUNKS - 2)
    stage_across(CHUNKS - 3)
    stage_direct(CHUNKS - 1)
    correlate(1)
    stage_forward(CHUNKS - 1)
    stage_across(CHUNKS - 2)
    correlate(2)
    stage_across(CHUNKS - 1)
    final()

    def finish(j, carry):
        some = send.at[j, pl.ds(0, GROUPS - 1)]
        pltpu.make_async_copy(some, some, a2a_s.at[j]).wait()
        for part in range(3):
            direct(j, part).wait_send()
        for way in range(2):
            for whole in range(2):
                forward(j, way, whole).wait_send()
        for which in range(4):
            share(j, which).wait_send()
        return carry

    lax.fori_loop(0, CHUNKS, finish, 0)
    for slot in range(2):
        for piece in range(len(PIECES[slot]) - 1):
            deliver(slot, piece).wait_send()
            deliver(slot, piece).wait_recv()


def shards(samples, fir_taps, channel_group, tile_pairs):
    slots = tile_pairs.shape[1]
    pieces = len(PIECES[0]) - 1
    tables = jnp.asarray(twiddle_tables())
    dma = pltpu.SemaphoreType.DMA
    any_spec = pl.BlockSpec(memory_space=pl.ANY)
    vmem = pl.BlockSpec(memory_space=pltpu.VMEM)
    smem = pl.BlockSpec(memory_space=pltpu.SMEM)
    return pl.pallas_call(
        kernel,
        out_shape=pltpu.VMEM((ROWS, slots, 2, BLOCK, BLOCK), jnp.bfloat16),
        in_specs=[any_spec, any_spec, any_spec, vmem, any_spec, smem],
        out_specs=vmem,
        scratch_shapes=[
            pltpu.VMEM((CHUNKS, TRI, 3, NBLK, DISH, 128), jnp.bfloat16),
            pltpu.VMEM((CHUNKS, ROWS, NBLK, DISH, 128), jnp.bfloat16),
            pltpu.VMEM((2, 2, slots), jnp.int32),
            pltpu.SMEM((2, 2, slots), jnp.int32),
            pltpu.VMEM((DISH, RING * FSTEP * NFFT), jnp.bfloat16),
            pltpu.VMEM(fir_taps.shape, jnp.float32),
            pltpu.VMEM(tables.shape, jnp.bfloat16),
            pltpu.VMEM((CHANNELS, CHANNELS), jnp.bfloat16),
            pltpu.VMEM((RADIX, MROWS, 128), jnp.float32),
            pltpu.VMEM((MROWS, NFFT), jnp.bfloat16),
            pltpu.VMEM((2 * MROWS, CHANNELS), jnp.bfloat16),
            pltpu.VMEM((CHUNKS, GROUPS, ROWS, DISH, 128), jnp.bfloat16),
            pltpu.VMEM((2, NBLK, BLOCK, 256), jnp.bfloat16),
            pltpu.VMEM((2, NBLK, 256, 256), jnp.bfloat16),
            pltpu.VMEM((4, slots, BLOCK, 256), jnp.float32),
            pltpu.VMEM((slots, 2, BLOCK, BLOCK), jnp.bfloat16),
            dma((CHUNKS + 2,)), dma((2,)), dma((2, pieces)), dma((2, pieces)), dma((2,)), dma((2,)), dma((2,)),
            dma((2, CHUNKS)), dma((CHUNKS,)), dma((CHUNKS,)),
            dma((3, CHUNKS)), dma((3, CHUNKS)), dma((2, 2, CHUNKS)), dma((2, 2, CHUNKS)),
            dma((4, CHUNKS)), dma((4, CHUNKS)),
        ],
        compiler_params=pltpu.CompilerParams(
            collective_id=0, has_side_effects=True, vmem_limit_bytes=56 << 20),
        name="correlator",
    )(samples, fir_taps, tables, channel_group.reshape(1, CHANNELS), tile_pairs, tile_pairs)


def solution(mesh):
    in_specs = (P(("grp", "tri"), None), P(), P(), P(None, "tri"))
    out_specs = P("grp", "tri", None, None, None)
    return jax.shard_map(shards, mesh=mesh, in_specs=in_specs, out_specs=out_specs, check_vma=False)
```

```python
import math

import jax
import jax.numpy as jnp
import numpy as np
from jax import lax
from jax.experimental import pallas as pl
from jax.experimental.pallas import tpu as pltpu
from jax.sharding import PartitionSpec as P

NFFT = 8192
TAPS = 16
BLOCK = 128
FIRST_CH = 1024
CHANNELS = 512
CH_GRP = 32
FAVG = 8
SPECTRA = 64
NBLK = 16
DISH = 16
GROUPS = 16
TRI = 8
ROWS = CH_GRP // FAVG
FSTEP = 8
CHUNKS = SPECTRA // FSTEP
MROWS = FSTEP * DISH
FAR = (range(0, 9), range(9, 17))
PIECES = ((0, 2, 5, 9), (9, 11, 13, 17))
RING = 4
RADIX = 8
SUB = NFFT // RADIX
RESIDUES = (0, 4, 1, 7, 2, 6, 3, 5)
MESH = pl.DeviceIdType.MESH


def twiddle_tables():
    n = np.arange(SUB, dtype=np.int64)[:, None]
    k2 = np.arange(CHANNELS // RADIX, dtype=np.int64)[None, :]
    scale = 1.0 / math.sqrt(NFFT)
    tables = np.zeros((4, 2 * SUB, 256), np.float64)
    for pair in range(4):
        for which in range(2):
            residue = RESIDUES[2 * pair + which]
            channel = FIRST_CH + RADIX * k2 + residue
            angle = ((n * channel) % NFFT) * (2.0 * math.pi / NFFT)
            cos, sin = np.cos(angle) * scale, np.sin(angle) * scale
            re, im = slice(which * 64, which * 64 + 64), slice(128 + which * 64, 192 + which * 64)
            if pair == 0:
                rows = slice(which * SUB, (which + 1) * SUB)
                tables[pair, rows, re] = cos
                tables[pair, rows, im] = -sin
            else:
                sign = 1.0 if which == 0 else -1.0
                tables[pair, :SUB, re] = cos
                tables[pair, SUB:, re] = -sign * sin
                tables[pair, :SUB, im] = -sin
                tables[pair, SUB:, im] = -sign * cos
    return tables.astype(jnp.bfloat16)


def al(x):
    return pl.multiple_of(x, 128)


def kernel(
    samples, taps, tables, group_row, pairs, own_pairs, out,
    volts, mine4, pairs_in, near_pairs, xs, fir, wt, perm, fbuf, planes, spec, send, rows, cols, acc, stage,
    x_sem, w_sem, o_s, o_r, p_s, p_r, p_l, own_sem, a2a_s, a2a_r, dir_s, dir_r, fwd_s, fwd_r, sib_s, sib_r,
):
    grp, tri = lax.axis_index("grp"), lax.axis_index("tri")
    gy, gz = grp // 4, lax.rem(grp, 4)
    cx, core = tri // 2, lax.rem(tri, 2)
    slots = own_pairs.shape[1]
    last = CHUNKS // 2 - 1

    def group_at(dy, dz):
        return lax.rem(gy + dy, 4) * 4 + lax.rem(gz + dz, 4)

    def tri_at(dx):
        return lax.rem(cx + dx, 4) * 2 + core

    partners = [group_at(dy, dz) for dy in range(4) for dz in range(4) if (dy, dz) != (0, 0)]
    right, left, across = tri_at(1), tri_at(3), tri_at(2)
    sibling = cx * 2 + (1 - core)

    def frames_copy(i, count):
        src = pl.ds(al(i * (FSTEP * NFFT)), count * NFFT)
        dst = pl.ds(al(lax.rem(i, RING) * (FSTEP * NFFT)), count * NFFT)
        return pltpu.make_async_copy(samples.at[:, src], xs.at[:, dst], x_sem.at[i])

    table_copy = pltpu.make_async_copy(tables, wt, w_sem.at[0])
    taps_copy = pltpu.make_async_copy(taps, fir, w_sem.at[1])
    taps_copy.start()
    for i in range(3):
        frames_copy(i, FSTEP).start()

    barrier = pltpu.get_barrier_semaphore()
    for p in partners:
        pl.semaphore_signal(barrier, inc=1, device_id=(p, tri), device_id_type=MESH)
    for t in (right, left, sibling):
        pl.semaphore_signal(barrier, inc=1, device_id=(grp, t), device_id_type=MESH)

    number = lax.broadcasted_iota(jnp.int32, (64, CHANNELS), 1)
    for piece in range(RADIX):
        channel = lax.broadcasted_iota(jnp.int32, (64, CHANNELS), 0) * RADIX + RESIDUES[piece]
        groups = jnp.broadcast_to(group_row[...], (64, CHANNELS))
        mine = jnp.sum(jnp.where(number == channel, groups, 0), axis=1, keepdims=True)
        before = jnp.where((groups == mine) & (number < channel), 1, 0)
        rank = jnp.sum(before, axis=1, keepdims=True)
        one = jnp.where(number == mine * CH_GRP + rank, 1.0, 0.0)
        perm[pl.ds(piece * 64, 64), :] = one.astype(jnp.bfloat16)

    def a2a_copy(j, i):
        p = partners[i]
        return pltpu.make_async_remote_copy(
            src_ref=send.at[j, p], dst_ref=mine4.at[j, grp],
            send_sem=a2a_s.at[j], recv_sem=a2a_r.at[j],
            device_id=(p, tri), device_id_type=MESH)

    def own_copy(j):
        return pltpu.make_async_copy(send.at[j, grp], mine4.at[j, grp], own_sem.at[0, j])

    def keep_copy(j):
        return pltpu.make_async_copy(mine4.at[j, :, pl.ds(1, 3)], volts.at[j, tri], own_sem.at[1, j])

    def remote(src, dst, to, ssem, rsem):
        return pltpu.make_async_remote_copy(
            src_ref=src, dst_ref=dst, send_sem=ssem, recv_sem=rsem,
            device_id=(grp, to), device_id_type=MESH)

    def direct(j, part):
        if part == 0:
            src, dst, way = mine4.at[j, :, pl.ds(2, 2)], volts.at[j, tri, :, pl.ds(0, 2)], 0
        elif part == 1:
            src, dst, way = mine4.at[j, :, 0], volts.at[j, tri, :, 2], 0
        else:
            src, dst, way = mine4.at[j, :, pl.ds(0, 3)], volts.at[j, tri], 1
        return remote(src, dst, (right, left)[way], dir_s.at[part, j], dir_r.at[part, j])

    def forward(j, way, whole):
        t = (left, right)[way]
        if whole:
            src, dst = volts.at[j, t, :, 1], volts.at[j, t, :, 2 * way]
        else:
            half = pl.ds(8 * way, 8)
            src, dst = volts.at[j, t, half, 2 - 2 * way], volts.at[j, t, half, 1]
        return remote(src, dst, (right, left)[way], fwd_s.at[way, whole, j], fwd_r.at[way, whole, j])

    def share(j, which):
        t = (tri, left, right, across)[which]
        src = mine4.at[j, :, pl.ds(1, 3)] if which == 0 else volts.at[j, t]
        return remote(src, volts.at[j, t], sibling, sib_s.at[which, j], sib_r.at[which, j])

    def stage_direct(j):
        own_copy(j).wait()
        some = mine4.at[j, pl.ds(0, GROUPS - 1)]
        pltpu.make_async_copy(some, some, a2a_r.at[j]).wait()
        for part in (2, 0, 1):
            direct(j, part).start()
        share(j, 0).start()
        keep_copy(j).start()

    def stage_forward(j):
        direct(j, 2).wait_recv()
        for whole in (1, 0):
            forward(j, 1, whole).start()
        direct(j, 0).wait_recv()
        direct(j, 1).wait_recv()
        for whole in (1, 0):
            forward(j, 0, whole).start()
        share(j, 1).start()
        share(j, 2).start()

    def stage_across(j):
        for way in range(2):
            for whole in range(2):
                forward(j, way, whole).wait_recv()
        share(j, 3).start()

    half_root = math.sqrt(0.5)
    lane = lax.broadcasted_iota(jnp.int32, (DISH, 128), 1)

    def filter_tile(j, i):
        base = [lax.rem(j + k, RING) * (FSTEP * NFFT) for k in range(3)]
        for n1 in range(RADIX):
            off = n1 * SUB + i * 128
            coef = [fir[pl.ds(t, 1), pl.ds(al(off), 128)] for t in range(TAPS)]
            accs = [None] * FSTEP
            for fr in range(FSTEP + TAPS - 1):
                at = al(base[fr // FSTEP] + (fr % FSTEP) * NFFT + off)
                x = xs[:, pl.ds(at, 128)].astype(jnp.float32)
                for f in range(max(0, fr - TAPS + 1), min(FSTEP - 1, fr) + 1):
                    term = x * coef[fr - f]
                    accs[f] = term if accs[f] is None else accs[f] + term
                    if fr - f == TAPS - 1:
                        fbuf[n1, pl.ds(f * DISH, DISH), :] = accs[f]
        for f in range(FSTEP):
            at = pl.ds(f * DISH, DISH)
            v = [fbuf[n1, at, :] for n1 in range(RADIX)]
            a = [v[k] + v[k + 4] for k in range(4)]
            b = [v[k] - v[k + 4] for k in range(4)]
            even, odd = a[0] + a[2], a[1] + a[3]
            diff = (b[1] - b[3]) * half_root
            total = (b[1] + b[3]) * half_root
            res = (even + odd, even - odd, b[0] + diff, b[2] + total,
                   a[0] - a[2], a[1] - a[3], b[0] - diff, total - b[2])
            for k in range(RADIX):
                planes[at, pl.ds(al(k * SUB + i * 128), 128)] = res[k].astype(jnp.bfloat16)

    def transform(j):
        for p in range(4):
            got = jnp.dot(planes[:, p * 2048 : (p + 1) * 2048], wt[p], preferred_element_type=jnp.float32)
            got = got.astype(jnp.bfloat16)
            for part in range(2):
                spec[part * MROWS : (part + 1) * MROWS, p * 128 : (p + 1) * 128] = got[:, part * 128 : (part + 1) * 128]
        for two in range(2):
            sorted_ = jnp.dot(spec[...], perm[:, two * 256 : (two + 1) * 256], preferred_element_type=jnp.float32)
            for one in range(2):
                blk = sorted_[:, one * 128 : (one + 1) * 128]
                t = []
                for k in range(2 * FSTEP):
                    v = blk[k * DISH : (k + 1) * DISH]
                    t.append(pltpu.roll(v, 8 * k, 1) if k else v)
                for bit in range(4):
                    odd = (lane >> (3 + bit)) & 1 == 1
                    t = [jnp.where(odd, t[(k + (1 << bit)) % 16], t[k]) for k in range(16)]
                for go in range(16):
                    send[j, two * 8 + one * 4 + go // 4, lax.rem(go % 4 + 6 - cx, 4)] = t[-go % 16].astype(jnp.bfloat16)

    def arrived(k):
        for j in (2 * k, 2 * k + 1):
            keep_copy(j).wait()
            for which in range(4):
                share(j, which).wait_recv()

    def arrange(k, r, slot):
        go = lax.rem(grp, 4) * 4 + lax.rem(cx + 3 + r, 4)
        place = lax.rem((lax.broadcasted_iota(jnp.int32, (BLOCK, BLOCK), 0) >> 3) - go + 16, 16)
        sign = jnp.where(place < FSTEP, -1.0, 1.0).astype(jnp.bfloat16)

        def block(b, c):
            for h in range(2):
                v = volts[2 * k + h, :, b, r].reshape(BLOCK, 128)
                rows[slot, b, :, h * 128 : (h + 1) * 128] = v
                vt = v.T
                cols[slot, b, h * 128 : (h + 1) * 128, 0:128] = vt
                swapped = jnp.concatenate([vt[64:], vt[:64]], axis=0)
                cols[slot, b, h * 128 : (h + 1) * 128, 128:256] = swapped * sign
            return c

        lax.fori_loop(0, NBLK, block, 0, unroll=4)

    def product(slot, ref, s):
        return jnp.dot(rows[slot, ref[0, s]], cols[slot, ref[1, s]], preferred_element_type=jnp.float32)

    def correlate(k):
        arrived(k)

        def add(r, slot, ref, s):
            got = product(slot, ref, s)
            acc[r, s] = got if k == 0 else got + acc[r, s]

        for r, slot in ((0, 0), (2, 1), (1, 0)):
            arrange(k, r, slot)
            for s in range(slots):
                add(r, slot, own_pairs, s)
            if r != 1:
                for s in FAR[slot]:
                    add(3, slot, near_pairs.at[slot], s)

    def result(r, slot, ref, s):
        got = (product(slot, ref, s) + acc[r, s]) * (1.0 / (SPECTRA * FAVG))
        return got.astype(jnp.bfloat16)

    def deliver(slot, piece):
        lo, hi = PIECES[slot][piece], PIECES[slot][piece + 1]
        part = pl.ds(lo, hi - lo)
        return remote(stage.at[part], out.at[lax.rem(cx + 3 + 2 * slot, 4), part], (right, left)[slot],
                      o_s.at[slot, piece], o_r.at[slot, piece])

    def final():
        arrived(last)
        for slot in range(2):
            arrange(last, 2 * slot, slot)
            for piece in range(len(PIECES[slot]) - 1):
                for s in range(PIECES[slot][piece], PIECES[slot][piece + 1]):
                    got = result(3, slot, near_pairs.at[slot], s)
                    for part in range(2):
                        stage[s, part] = got[:, part * 128 : (part + 1) * 128]
                deliver(slot, piece).start()
        for r, slot in ((0, 0), (2, 1), (1, 0)):
            if r == 1:
                arrange(last, r, slot)
            row = lax.rem(cx + 3 + r, 4)
            for s in range(slots):
                got = result(r, slot, own_pairs, s)
                for part in range(2):
                    out[row, s, part] = got[:, part * 128 : (part + 1) * 128]

    def pairs_copy(way):
        return remote(pairs, pairs_in.at[way], (left, right)[way], p_s.at[way], p_r.at[way])

    def tiles(s, send_previous):
        def tile(i, c):
            filter_tile(s, i)
            return c

        lax.fori_loop(0, SUB // 128, tile, 0)

    def ship(s):
        transform(s)
        for i in range(GROUPS - 1):
            a2a_copy(s, i).start()
        own_copy(s).start()

    taps_copy.wait()
    for i in range(3):
        frames_copy(i, FSTEP).wait()
    table_copy.start()
    frames_copy(3, FSTEP).start()
    tiles(0, False)
    pl.semaphore_wait(barrier, len(partners) + 3)
    table_copy.wait()
    for way in range(2):
        pairs_copy(way).start()
    ship(0)

    def step(s, carry):
        @pl.when(s + 3 < CHUNKS + 1)
        def _():
            frames_copy(s + 3, FSTEP).start()

        @pl.when(s + 3 == CHUNKS + 1)
        def _():
            frames_copy(CHUNKS + 1, FSTEP - 1).start()

        @pl.when(s + 2 < CHUNKS + 1)
        def _():
            frames_copy(s + 2, FSTEP).wait()

        @pl.when(s + 2 == CHUNKS + 1)
        def _():
            frames_copy(CHUNKS + 1, FSTEP - 1).wait()

        tiles(s, True)
        stage_direct(s - 1)

        ship(s)

        @pl.when(s >= 2)
        def _():
            stage_forward(s - 2)

        @pl.when(s >= 3)
        def _():
            stage_across(s - 3)

        return carry

    lax.fori_loop(1, CHUNKS, step, 0)
    for way in range(2):
        pairs_copy(way).wait()
        pltpu.make_async_copy(pairs_in.at[way], near_pairs.at[way], p_l.at[way]).start()
    for way in range(2):
        pltpu.make_async_copy(pairs_in.at[way], near_pairs.at[way], p_l.at[way]).wait()
    correlate(0)
    stage_forward(CHUNKS - 2)
    stage_across(CHUNKS - 3)
    stage_direct(CHUNKS - 1)
    correlate(1)
    stage_forward(CHUNKS - 1)
    stage_across(CHUNKS - 2)
    correlate(2)
    stage_across(CHUNKS - 1)
    final()

    def finish(j, carry):
        some = send.at[j, pl.ds(0, GROUPS - 1)]
        pltpu.make_async_copy(some, some, a2a_s.at[j]).wait()
        for part in range(3):
            direct(j, part).wait_send()
        for way in range(2):
            for whole in range(2):
                forward(j, way, whole).wait_send()
        for which in range(4):
            share(j, which).wait_send()
        return carry

    lax.fori_loop(0, CHUNKS, finish, 0)
    for slot in range(2):
        for piece in range(len(PIECES[slot]) - 1):
            deliver(slot, piece).wait_send()
            deliver(slot, piece).wait_recv()


def shards(samples, fir_taps, channel_group, tile_pairs):
    slots = tile_pairs.shape[1]
    pieces = len(PIECES[0]) - 1
    tables = jnp.asarray(twiddle_tables())
    dma = pltpu.SemaphoreType.DMA
    any_spec = pl.BlockSpec(memory_space=pl.ANY)
    vmem = pl.BlockSpec(memory_space=pltpu.VMEM)
    smem = pl.BlockSpec(memory_space=pltpu.SMEM)
    return pl.pallas_call(
        kernel,
        out_shape=pltpu.VMEM((ROWS, slots, 2, BLOCK, BLOCK), jnp.bfloat16),
        in_specs=[any_spec, any_spec, any_spec, vmem, any_spec, smem],
        out_specs=vmem,
        scratch_shapes=[
            pltpu.VMEM((CHUNKS, TRI, NBLK, 3, DISH, 128), jnp.bfloat16),
            pltpu.VMEM((CHUNKS, NBLK, ROWS, DISH, 128), jnp.bfloat16),
            pltpu.VMEM((2, 2, slots), jnp.int32),
            pltpu.SMEM((2, 2, slots), jnp.int32),
            pltpu.VMEM((DISH, RING * FSTEP * NFFT), jnp.bfloat16),
            pltpu.VMEM(fir_taps.shape, jnp.float32),
            pltpu.VMEM(tables.shape, jnp.bfloat16),
            pltpu.VMEM((CHANNELS, CHANNELS), jnp.bfloat16),
            pltpu.VMEM((RADIX, MROWS, 128), jnp.float32),
            pltpu.VMEM((MROWS, NFFT), jnp.bfloat16),
            pltpu.VMEM((2 * MROWS, CHANNELS), jnp.bfloat16),
            pltpu.VMEM((CHUNKS, GROUPS, ROWS, DISH, 128), jnp.bfloat16),
            pltpu.VMEM((2, NBLK, BLOCK, 256), jnp.bfloat16),
            pltpu.VMEM((2, NBLK, 256, 256), jnp.bfloat16),
            pltpu.VMEM((4, slots, BLOCK, 256), jnp.float32),
            pltpu.VMEM((slots, 2, BLOCK, BLOCK), jnp.bfloat16),
            dma((CHUNKS + 2,)), dma((2,)), dma((2, pieces)), dma((2, pieces)), dma((2,)), dma((2,)), dma((2,)),
            dma((2, CHUNKS)), dma((CHUNKS,)), dma((CHUNKS,)),
            dma((3, CHUNKS)), dma((3, CHUNKS)), dma((2, 2, CHUNKS)), dma((2, 2, CHUNKS)),
            dma((4, CHUNKS)), dma((4, CHUNKS)),
        ],
        compiler_params=pltpu.CompilerParams(
            collective_id=0, has_side_effects=True, vmem_limit_bytes=56 << 20),
        name="correlator",
    )(samples, fir_taps, tables, channel_group.reshape(1, CHANNELS), tile_pairs, tile_pairs)


def solution(mesh):
    in_specs = (P(("grp", "tri"), None), P(), P(), P(None, "tri"))
    out_specs = P("grp", "tri", None, None, None)
    return jax.shard_map(shards, mesh=mesh, in_specs=in_specs, out_specs=out_specs, check_vma=False)
```
